32 devices in a mesh: ctx: 16 (over z, y, x), tp: 2 (over core).
Axes of the slice: x: 2, y: 2, z: 4, core: 2. Of those that a mesh axis runs over, the one named last changes fastest.
Arguments:
- queries: bfloat16 [12288, 2048], P('ctx', 'tp'), may hold values from -9 to 9
- keys: bfloat16 [12288, 2048], P('ctx', 'tp'), may hold values from -130 to 130
- values: bfloat16 [12288, 2048], P('ctx', 'tp'), may hold values from -6 to 6
- residual: bfloat16 [12288, 3072], P('ctx', 'tp'), may hold values from -3 to 3
- gate: float32 [3072], P('tp'), may hold values from 1 to 4
- out_weight: bfloat16 [2048, 3072], P('tp'), may hold values from -0.1875 to 0.1875
Outputs:
- mixed: bfloat16 [12288, 3072], P('ctx', 'tp')
The draws below stay inside these ranges and needn't reach their ends.
All inputs are finite; a program needn't handle non-finite values.
Results may differ from the reference program's by a relative error of at most 0.014.
Values may be sent and summed in bfloat16 or wider, within the bound.
No kernel may reach another device: no remote copies, remote signals or barrier semaphores. Data moves between devices by JAX's collectives and lax.ppermute only.
A program may use at most 128 MiB of HBM per device.

```python
import jax
import jax.numpy as jnp
from jax import lax

D = 3072
HEADS = 16
HEAD_DIM = 128
TOK_DEV = 768
CYCLE = 8
SEQS = 2
TOKENS = 12288
N_TP = 2


def joint_draw(key):
    width_all = HEADS * HEAD_DIM
    query_full = jnp.clip(1.5 * jax.random.normal(jax.random.fold_in(key, 11), (TOKENS, width_all), jnp.float32), -9.0, 9.0)
    key_full = jnp.clip(1.5 * jax.random.normal(jax.random.fold_in(key, 12), (TOKENS, width_all), jnp.float32), -9.0, 9.0)
    return (query_full, key_full)


def draw_queries(key, part):
    return joint_draw(key)[0].astype(jnp.bfloat16)


def draw_keys(key, part):
    return joint_draw(key)[1].astype(jnp.bfloat16)


def with_spikes(drawn, own_key, source, target, parts, factor):
    def block_of(dim):
        return (jnp.arange(drawn.shape[dim]) // (drawn.shape[dim] // parts)).reshape((-1,) + (1,) * (drawn.ndim - 1 - dim))

    near = jax.random.permutation(own_key, parts)[block_of(target)]
    second = (block_of(target) + parts // 2) % parts
    return jnp.where((block_of(source) == near) | (block_of(source) == second), factor * drawn, drawn)


def block_levels(key, dims, shards, least, largest):
    def one(position, blocks):
        heights = jax.random.uniform(jax.random.fold_in(jax.random.fold_in(key, 6), position), (blocks,), jnp.float32, least / len(shards), largest / len(shards))
        return jnp.repeat(jnp.exp(heights), dims[position] // blocks).reshape((-1,) + (1,) * (len(dims) - position - 1))

    gain = one(*shards[0])
    for cut in shards[1:]:
        gain = gain * one(*cut)
    return gain


def bell_draw(rng, dims, width, limit, cuts=(), held_as=jnp.bfloat16):
    level = block_levels(rng, dims, cuts, -0.22, 0.18) if cuts else 1.0
    values = jax.random.normal(rng, dims, jnp.float32) * width * level
    return jnp.minimum(jnp.maximum(values, -limit), limit).astype(held_as)


def heavy_noise(key, shape, deviation, most, split, heavy, held_as=jnp.bfloat16):
    values = deviation * jax.random.normal(key, shape, jnp.float32)
    if split:
        values = values * block_levels(key, shape, split, -0.22, 0.18)
    return jnp.clip(with_spikes(values, jax.random.fold_in(key, 3), *heavy), -most, most).astype(held_as)


def setup_inputs(seed: int = 0) -> dict:
    key_list = jax.random.split(jax.random.key(seed), 7)
    queries = draw_queries(jax.random.fold_in(key_list[6], 71), 0)
    keys = draw_keys(jax.random.fold_in(key_list[6], 71), 0)
    values = bell_draw(key_list[2], (TOKENS, HEADS * HEAD_DIM), 1.0, 6.0, ((0, 16), (1, 2)))
    residual = bell_draw(key_list[3], (TOKENS, D), 0.5, 3.0, ((0, 16), (1, 2)))
    gate = jnp.clip(1.0 + 3.0 * jax.random.uniform(key_list[4], (D,), jnp.float32) ** block_levels(key_list[4], (D,), ((0, 2),), -0.2, 0.2), 1.0, 4.0)
    out_weight = heavy_noise(key_list[5], (HEADS * HEAD_DIM, D), (HEADS * HEAD_DIM) ** -0.5, 0.1875, ((0, 2),), (0, 1, 2, 2.0))
    return {"queries": queries, "keys": keys, "values": values, "residual": residual, "gate": gate, "out_weight": out_weight}


def arrange(array):
    shaped = array.reshape(CYCLE, SEQS, TOK_DEV, HEADS, HEAD_DIM)
    return shaped.transpose(1, 0, 2, 3, 4).reshape(SEQS, CYCLE * TOK_DEV, HEADS, HEAD_DIM)


def reference(queries, keys, values, residual, gate, out_weight):
    length = CYCLE * TOK_DEV
    width_all = HEADS * HEAD_DIM
    scale = 1.0 / (HEAD_DIM ** 0.5)
    query_seq = arrange(queries)
    key_seq = arrange(keys)
    value_seq = arrange(values)
    block = min(512, length)
    blocks = length // block

    def one_block(index):
        seq_index = index // blocks
        block_index = index % blocks
        query_all = lax.dynamic_index_in_dim(query_seq, seq_index, 0, keepdims=False)
        query_block = lax.dynamic_slice_in_dim(query_all, (block_index * block).astype(jnp.int32), block, 0)
        key_all = lax.dynamic_index_in_dim(key_seq, seq_index, 0, keepdims=False)
        value_all = lax.dynamic_index_in_dim(value_seq, seq_index, 0, keepdims=False)
        scores = jnp.einsum("qhd,khd->hqk", query_block.astype(jnp.float32), key_all.astype(jnp.float32)) * scale
        top = jnp.max(scores, axis=-1, keepdims=True)
        weights = jnp.exp(scores - top)
        total = jnp.sum(weights, axis=-1)
        rounded = lax.optimization_barrier(weights.astype(jnp.bfloat16)).astype(jnp.float32)
        summed = jnp.einsum("hqk,khd->qhd", rounded, value_all.astype(jnp.float32))
        return (summed / total.T[:, :, None]).astype(jnp.bfloat16)

    result = lax.map(one_block, jnp.arange(SEQS * blocks, dtype=jnp.int32))
    result = result.reshape(SEQS, CYCLE, TOK_DEV, HEADS, HEAD_DIM).transpose(1, 0, 2, 3, 4)
    attended = result.reshape(TOKENS, width_all)
    group = width_all // N_TP

    def add_group(counter, accum):
        start = (counter * group).astype(jnp.int32)
        columns = lax.dynamic_slice_in_dim(attended, start, group, 1)
        rows = lax.dynamic_slice_in_dim(out_weight, start, group, 0)
        partial_value = jnp.dot(columns, rows, preferred_element_type=jnp.float32)
        return accum + lax.optimization_barrier(partial_value.astype(jnp.bfloat16)).astype(jnp.float32)

    projected = lax.fori_loop(0, N_TP, add_group, jnp.zeros((TOKENS, D), jnp.float32))
    return (residual.astype(jnp.float32) + gate[None, :] * projected).astype(jnp.bfloat16)
```

```python
import functools
import math

import jax
import jax.numpy as jnp
from jax import lax
from jax.experimental import pallas as pl
from jax.experimental.pallas import tpu as pltpu
from jax.sharding import PartitionSpec as P

HEAD_DIM = 128
CYCLE = 8
SCALE = math.log2(math.e) / math.sqrt(HEAD_DIM)
MIB = 2**20


def passed_along(array, axis, by):
    length = lax.axis_size(axis)
    return lax.ppermute(array, axis, [(i, (i + by) % length) for i in range(length)])


def swapped(array, mask):
    length = lax.axis_size("ctx")
    groups = length // CYCLE
    pairs = [(i, ((i // groups) ^ mask) * groups + i % groups) for i in range(length)]
    return lax.ppermute(array, "ctx", pairs)


def dot_nt(a, b):
    return lax.dot_general(a, b, (((1,), (1,)), ((), ())), preferred_element_type=jnp.float32)


def dot_nn(a, b):
    return lax.dot_general(a, b, (((1,), (0,)), ((), ())), preferred_element_type=jnp.float32)


def attend_kernel(tile, chunk, q_ref, *refs):
    pairs, (o_ref, kd, vx) = refs[:CYCLE], refs[CYCLE:]
    rows = pairs[0].shape[0]
    for i, pair in enumerate(pairs):
        span = pl.ds(i * rows, rows)
        kd[span, :HEAD_DIM] = pair[:, :HEAD_DIM]
        kd[span, HEAD_DIM:] = pair[:, :HEAD_DIM]
        vx[span, :HEAD_DIM] = pair[:, HEAD_DIM:]
        vx[span, HEAD_DIM:] = jnp.ones((rows, HEAD_DIM), jnp.bfloat16)
    steps = CYCLE * rows // chunk

    def one_tile(t, carry):
        span = pl.ds(pl.multiple_of(t * tile, tile), tile)
        scaled = q_ref[span, :].astype(jnp.float32) * SCALE
        high = scaled.astype(jnp.bfloat16)
        low = (scaled - high.astype(jnp.float32)).astype(jnp.bfloat16)
        both = jnp.concatenate([high, low], axis=1)
        upcoming = dot_nt(both, kd[pl.ds(0, chunk), :])
        top = total = None
        for i in range(steps):
            scores = upcoming
            if i + 1 < steps:
                upcoming = dot_nt(both, kd[pl.ds((i + 1) * chunk, chunk), :])
            largest = jnp.max(scores, axis=1, keepdims=True)
            newtop = largest if i == 0 else jnp.maximum(top, largest)
            weights = jnp.exp2(scores - newtop).astype(jnp.bfloat16)
            update = dot_nn(weights, vx[pl.ds(i * chunk, chunk), :])
            total = update if i == 0 else total * jnp.exp2(top - newtop) + update
            top = newtop
        o_ref[span, :] = (total[:, :HEAD_DIM] / total[:, HEAD_DIM:]).astype(jnp.bfloat16)
        return carry

    lax.fori_loop(0, q_ref.shape[0] // tile, one_tile, 0)


def attend(query, pairs):
    rows = pairs[0].shape[0]
    work = query.shape[0] * CYCLE * rows
    return pl.pallas_call(
        functools.partial(attend_kernel, rows, rows),
        out_shape=jax.ShapeDtypeStruct(query.shape, jnp.bfloat16),
        scratch_shapes=[pltpu.VMEM((CYCLE * rows, 2 * HEAD_DIM), jnp.bfloat16)] * 2,
        compiler_params=pltpu.CompilerParams(vmem_limit_bytes=48 * MIB),
        cost_estimate=pl.CostEstimate(
            flops=8 * HEAD_DIM * work, bytes_accessed=6 * MIB, transcendentals=work
        ),
    )(query, *pairs)


def by_heads(queries, keys, values, out_weight):
    rows_here = queries.shape[0]
    place = lax.axis_index("ctx") // (lax.axis_size("ctx") // CYCLE)

    def columns(array, mask):
        start = (place ^ mask) * HEAD_DIM
        return lax.dynamic_slice(array, (0, start), (rows_here, HEAD_DIM))

    pairs = {}
    for mask in (4, 5, 6, 7, 1, 2, 3):
        pair = jnp.concatenate([columns(keys, mask), columns(values, mask)], axis=1)
        pairs[mask] = swapped(pair, mask)
    query_of = {0: columns(queries, 0)}
    for mask in (4, 5, 6, 7, 1, 2, 3):
        query_of[mask] = swapped(columns(queries, mask), mask)
    pairs[0] = jnp.concatenate([columns(keys, 0), columns(values, 0)], axis=1)
    pair_list = [pairs[mask] for mask in range(CYCLE)]
    back = {}
    for mask in (4, 5, 6, 7, 1, 2, 3):
        back[mask] = swapped(attend(query_of[mask], pair_list), mask)
    back[0] = attend(query_of[0], pair_list)
    weight_rows = out_weight.reshape(CYCLE, HEAD_DIM, out_weight.shape[1])
    weight_here = jnp.concatenate(
        [
            lax.dynamic_index_in_dim(weight_rows, place ^ mask, 0, keepdims=False)
            for mask in range(CYCLE)
        ],
        axis=0,
    )
    attended = jnp.concatenate([back[mask] for mask in range(CYCLE)], axis=1)
    return attended, weight_here


def absorb(state, block_pair, query_local):
    running, totals, accum = state
    rows_here = query_local.shape[0]
    heads_here = query_local.shape[1]
    key_block = block_pair[0].reshape(rows_here, heads_here, HEAD_DIM)
    value_block = block_pair[1].reshape(rows_here, heads_here, HEAD_DIM)
    scores = jnp.einsum(
        "qhd,khd->hqk", query_local, key_block, preferred_element_type=jnp.float32
    ) * (1.0 / HEAD_DIM**0.5)
    newmax = jnp.maximum(running, jnp.max(scores, axis=-1))
    correction = jnp.exp(running - newmax)
    weights = jnp.exp(scores - newmax[:, :, None])
    totals = totals * correction + jnp.sum(weights, axis=-1)
    update = jnp.einsum(
        "hqk,khd->qhd",
        weights.astype(jnp.bfloat16),
        value_block,
        preferred_element_type=jnp.float32,
    )
    accum = accum * correction.T[:, :, None] + update
    return (newmax, totals, accum)


def by_ring(queries, keys, values):
    rows_here = queries.shape[0]
    heads_here = queries.shape[1] // HEAD_DIM
    groups = lax.axis_size("ctx") // CYCLE
    query_local = queries.reshape(rows_here, heads_here, HEAD_DIM)
    own_pair = jnp.stack((keys, values))
    start_state = (
        jnp.full((heads_here, rows_here), -1e30, jnp.float32),
        jnp.zeros((heads_here, rows_here), jnp.float32),
        jnp.zeros((rows_here, heads_here, HEAD_DIM), jnp.float32),
    )
    state = absorb(start_state, own_pair, query_local)

    def both_step(counter, carry):
        inner, upward, downward = carry
        upward = passed_along(upward, "ctx", groups)
        downward = passed_along(downward, "ctx", -groups)
        inner = absorb(absorb(inner, upward, query_local), downward, query_local)
        return (inner, upward, downward)

    state, upward, _ = lax.fori_loop(0, CYCLE // 2 - 1, both_step, (state, own_pair, own_pair))
    opposite = passed_along(upward, "ctx", groups)
    state = absorb(state, opposite, query_local)
    running, totals, accum = state
    return (
        (accum / totals.T[:, :, None])
        .astype(jnp.bfloat16)
        .reshape(rows_here, heads_here * HEAD_DIM)
    )


def local(queries, keys, values, residual, gate, out_weight):
    if queries.shape[1] == CYCLE * HEAD_DIM:
        attended, weight_here = by_heads(queries, keys, values, out_weight)
    else:
        attended, weight_here = by_ring(queries, keys, values), out_weight
    projected = lax.psum_scatter(
        lax.dot_general(
            weight_here, attended, (((0,), (1,)), ((), ())), preferred_element_type=jnp.float32
        ).astype(jnp.bfloat16),
        "tp",
        scatter_dimension=0,
        tiled=True,
    ).astype(jnp.float32)
    return (residual.astype(jnp.float32) + gate[None, :] * projected.T).astype(jnp.bfloat16)


def solution(mesh):
    return jax.shard_map(
        local,
        mesh=mesh,
        in_specs=(
            P("ctx", "tp"),
            P("ctx", "tp"),
            P("ctx", "tp"),
            P("ctx", "tp"),
            P("tp"),
            P("tp", None),
        ),
        out_specs=P("ctx", "tp"),
        check_vma=False,
    )
```

```python
import functools
import math

import jax
import jax.numpy as jnp
from jax import lax
from jax.experimental import pallas as pl
from jax.experimental.pallas import tpu as pltpu
from jax.sharding import PartitionSpec as P

HEAD_DIM = 128
CYCLE = 8
NEAR = CYCLE // 2
FAR = (4, 5, 6, 7)
SCALE = math.log2(math.e) / math.sqrt(HEAD_DIM)
MIB = 2**20
COST = (0, 0, 2, 16, 16, 16, 0)


def passed_along(array, axis, by):
    length = lax.axis_size(axis)
    return lax.ppermute(array, axis, [(i, (i + by) % length) for i in range(length)])


def swapped(array, mask):
    length = lax.axis_size("ctx")
    groups = length // CYCLE
    pairs = [(i, ((i // groups) ^ mask) * groups + i % groups) for i in range(length)]
    return lax.ppermute(array, "ctx", pairs)


def dot_nt(a, b):
    return lax.dot_general(a, b, (((1,), (1,)), ((), ())), preferred_element_type=jnp.float32)


def dot_nn(a, b):
    return lax.dot_general(a, b, (((1,), (0,)), ((), ())), preferred_element_type=jnp.float32)


def extract_kernel(plan, stacked, place_ref, *refs):
    ins, outs = list(refs[: sum(len(picks) for _, picks in plan)]), refs[-1 if stacked else -len(plan) :]
    for number, (_, picks) in enumerate(plan):
        for slot in range(len(picks)):
            columns = slice(slot * HEAD_DIM, (slot + 1) * HEAD_DIM)
            if stacked:
                outs[0][number, :, columns] = ins.pop(0)[...]
            else:
                outs[number][:, columns] = ins.pop(0)[...]


def extract(place, sources, plan, after=(), stacked=False):
    rows = sources[0].shape[0]
    picked = [(sources[pick], head_of) for head_of, picks in plan for pick in picks]
    if stacked:
        shapes = [(len(plan), rows, len(plan[0][1]) * HEAD_DIM)]
    else:
        shapes = [(rows, len(picks) * HEAD_DIM) for _, picks in plan]
    return pl.pallas_call(
        functools.partial(extract_kernel, plan, stacked),
        name="extract",
        grid_spec=pltpu.PrefetchScalarGridSpec(
            num_scalar_prefetch=1,
            grid=(1,),
            in_specs=[
                pl.BlockSpec((rows, HEAD_DIM), lambda i, place_ref, f=head_of: (0, f(place_ref[0])))
                for _, head_of in picked
            ]
            + [pl.BlockSpec(memory_space=pl.ANY)] * len(after),
            out_specs=[
                pl.BlockSpec(shape, lambda i, place_ref, n=len(shape): (0,) * n) for shape in shapes
            ],
        ),
        out_shape=[jax.ShapeDtypeStruct(shape, jnp.bfloat16) for shape in shapes],
        cost_estimate=pl.CostEstimate(flops=0, bytes_accessed=0, transcendentals=0),
        compiler_params=pltpu.CompilerParams(vmem_limit_bytes=(56 if len(picked) > 1 else 16) * MIB),
    )(place, *[source for source, _ in picked], *after)


def attend_kernel(plan, first, resume, finish, extra, *refs):
    near_queries, far_queries, near_blocks, far_blocks = plan
    refs = list(refs)
    near = refs.pop(0)
    queries = [refs.pop(0) for _ in range(far_queries)]
    pairs = [refs.pop(0) for _ in range(far_blocks)]
    held = [refs.pop(0) for _ in range(2)] if resume else []
    del refs[:extra]
    *outs, both, kd, vx = refs
    rows = near.shape[1]
    count, blocks = near_queries + far_queries, near_blocks + far_blocks

    for i in range(blocks):
        if i < near_blocks:
            key_block = near[i, :, :HEAD_DIM]
            value_block = near[i, :, HEAD_DIM : 2 * HEAD_DIM]
        else:
            key_block = pairs[i - near_blocks][:, :HEAD_DIM]
            value_block = pairs[i - near_blocks][:, HEAD_DIM : 2 * HEAD_DIM]
        span = pl.ds(i * rows, rows)
        kd[span, :HEAD_DIM] = key_block
        kd[span, HEAD_DIM:] = key_block
        vx[span, :HEAD_DIM] = value_block
        vx[span, HEAD_DIM:] = jnp.ones((rows, HEAD_DIM), jnp.bfloat16)

    for j in range(count):
        if j < near_queries:
            query = near[j, :, 2 * HEAD_DIM :]
        else:
            query = queries[j - near_queries][:, -HEAD_DIM:]
        scaled = query.astype(jnp.float32) * SCALE
        high = scaled.astype(jnp.bfloat16)
        both[j, :, :HEAD_DIM] = high
        both[j, :, HEAD_DIM:] = (scaled - high.astype(jnp.float32)).astype(jnp.bfloat16)

    def one_query(j, carry):
        upcoming = dot_nt(both[j], kd[pl.ds(0, rows), :])
        top = jnp.max(held[0][first + j], axis=1, keepdims=True) if resume else None
        total = held[1][first + j] if resume else None
        for i in range(blocks):
            scores = upcoming
            if i + 1 < blocks:
                upcoming = dot_nt(both[j], kd[pl.ds((i + 1) * rows, rows), :])
            largest = jnp.max(scores, axis=1, keepdims=True)
            newtop = largest if top is None else jnp.maximum(top, largest)
            weights = jnp.exp2(scores - newtop).astype(jnp.bfloat16)
            update = dot_nn(weights, vx[pl.ds(i * rows, rows), :])
            total = update if top is None else total * jnp.exp2(top - newtop) + update
            top = newtop
        if finish:
            outs[0][j] = (total[:, :HEAD_DIM] / total[:, HEAD_DIM:]).astype(jnp.bfloat16)
        else:
            outs[0][j] = jnp.broadcast_to(top, (rows, HEAD_DIM))
            outs[1][j] = total
        return carry

    if count == 1:
        one_query(0, 0)
    else:
        lax.fori_loop(0, count, one_query, 0)


def attend(near, plan, queries=(), pairs=(), held=(), first=0, finish=True, after=(), cost=0):
    rows = near.shape[1]
    count, blocks = plan[0] + plan[1], plan[2] + plan[3]
    work = count * rows * blocks * rows
    if finish:
        shapes = [jax.ShapeDtypeStruct((count, rows, HEAD_DIM), jnp.bfloat16)]
    else:
        shapes = [
            jax.ShapeDtypeStruct((count, rows, HEAD_DIM), jnp.float32),
            jax.ShapeDtypeStruct((count, rows, 2 * HEAD_DIM), jnp.float32),
        ]
    return pl.pallas_call(
        functools.partial(attend_kernel, plan, first, bool(held), finish, len(after)),
        name="attend",
        out_shape=shapes,
        in_specs=[pl.BlockSpec(memory_space=pltpu.VMEM)] * (1 + len(queries) + len(pairs) + len(held))
        + [pl.BlockSpec(memory_space=pl.ANY)] * len(after),
        scratch_shapes=[pltpu.VMEM((count, rows, 2 * HEAD_DIM), jnp.bfloat16)]
        + [pltpu.VMEM((blocks * rows, 2 * HEAD_DIM), jnp.bfloat16)] * 2,
        compiler_params=pltpu.CompilerParams(vmem_limit_bytes=(20 if count == 1 else 26) * MIB),
        cost_estimate=pl.CostEstimate(
            flops=cost * HEAD_DIM * work, bytes_accessed=0, transcendentals=0
        ),
    )(near, *queries, *pairs, *held, *after)


def gather_kernel(heads, place_ref, core_ref, *refs):
    count = len(heads)
    own, other, (own_weight, other_weight, out) = refs[:count], refs[count : 2 * count], refs[2 * count :]
    total = None
    for pieces, weight in ((own, own_weight), (other, other_weight)):
        for n in range(0, count, 2):
            left = jnp.concatenate([piece[...] for piece in pieces[n : n + 2]], axis=1)
            starts = [pl.multiple_of(head(place_ref[0]) * HEAD_DIM, HEAD_DIM) for head in heads[n : n + 2]]
            right = jnp.concatenate([weight[pl.ds(start, HEAD_DIM), :] for start in starts], axis=0)
            product = dot_nn(left, right)
            total = product if total is None else total + product
    out[...] = total


def gather_heads(place, core, heads, own, other, out_weight, other_weight):
    rows, width = own[0][0].shape[1], out_weight.shape[1] // 2
    tile = width // 3
    pieces = [*own, *other]
    weight_spec = pl.BlockSpec(
        (out_weight.shape[0], tile), lambda c, place, core: (0, core[0] * 3 + c)
    )
    return pl.pallas_call(
        functools.partial(gather_kernel, heads),
        name="gather_heads",
        grid_spec=pltpu.PrefetchScalarGridSpec(
            num_scalar_prefetch=2,
            grid=(3,),
            in_specs=[
                pl.BlockSpec((None, rows, HEAD_DIM), lambda c, place, core, n=index: (n, 0, 0))
                for _, index in pieces
            ]
            + [weight_spec] * 2,
            out_specs=pl.BlockSpec((rows, tile), lambda c, place, core: (0, c)),
        ),
        out_shape=jax.ShapeDtypeStruct((rows, width), jnp.float32),
        compiler_params=pltpu.CompilerParams(vmem_limit_bytes=48 * MIB),
        cost_estimate=pl.CostEstimate(flops=0, bytes_accessed=0, transcendentals=0),
    )(place, core, *[array for array, _ in pieces], out_weight, other_weight)


def finish_kernel(place_ref, core_ref, own, other, own_rows, other_rows, before, residual, gate, out):
    left = jnp.concatenate([own[...], other[...]], axis=1)
    right = jnp.concatenate([own_rows[...], other_rows[...]], axis=0)
    total = before[...] + dot_nn(left, right)
    out[...] = (residual[...].astype(jnp.float32) + gate[...] * total).astype(out.dtype)


def finish(place, core, head, own, other, out_weight, other_weight, before, residual, gate):
    rows, width = residual.shape
    tile = width // 3
    piece = pl.BlockSpec((None, rows, HEAD_DIM), lambda c, place, core: (0, 0, 0))
    weight_rows = pl.BlockSpec(
        (HEAD_DIM, tile), lambda c, place, core: (head(place[0]), core[0] * 3 + c)
    )
    tiled = pl.BlockSpec((rows, tile), lambda c, place, core: (0, c))
    return pl.pallas_call(
        finish_kernel,
        name="finish",
        grid_spec=pltpu.PrefetchScalarGridSpec(
            num_scalar_prefetch=2,
            grid=(3,),
            in_specs=[piece] * 2
            + [weight_rows] * 2
            + [tiled] * 2
            + [pl.BlockSpec((1, tile), lambda c, place, core: (0, c))],
            out_specs=tiled,
        ),
        out_shape=jax.ShapeDtypeStruct((rows, width), jnp.bfloat16),
        compiler_params=pltpu.CompilerParams(vmem_limit_bytes=40 * MIB),
        cost_estimate=pl.CostEstimate(flops=0, bytes_accessed=0, transcendentals=0),
    )(place, core, own, other, out_weight, other_weight, before, residual, gate.reshape(1, -1))


def joined_kernel(count, *refs):
    for i in range(count):
        refs[-1][i] = refs[i][0]


def joined(pieces, after):
    shape = (len(pieces), *pieces[0].shape[1:])
    return pl.pallas_call(
        functools.partial(joined_kernel, len(pieces)),
        name="joined",
        in_specs=[pl.BlockSpec(memory_space=pltpu.VMEM)] * len(pieces)
        + [pl.BlockSpec(memory_space=pl.ANY)] * len(after),
        out_shape=jax.ShapeDtypeStruct(shape, pieces[0].dtype),
        compiler_params=pltpu.CompilerParams(vmem_limit_bytes=16 * MIB),
        cost_estimate=pl.CostEstimate(flops=0, bytes_accessed=0, transcendentals=0),
    )(*pieces, *after)


def to_partner(array):
    return lax.ppermute(array, "tp", [(0, 1), (1, 0)])


def by_heads(queries, keys, values, residual, gate, out_weight):
    length = lax.axis_size("ctx")
    groups = length // CYCLE
    place = (lax.axis_index("ctx") // groups).reshape(1).astype(jnp.int32)
    core = lax.axis_index("tp").reshape(1).astype(jnp.int32)
    sources = (keys, values, queries)
    near_groups = [
        [(half * NEAR + i) * groups + g for i in range(NEAR)] for half in (0, 1) for g in range(groups)
    ]

    def of_mask(mask):
        return lambda p: p ^ mask

    def exchanged(array):
        return lax.all_to_all(array, "ctx", 0, 0, axis_index_groups=near_groups, tiled=True)

    def far_exchange(masks, picks, after=()):
        pieces = extract(place, sources, [(of_mask(mask), picks) for mask in masks], after)
        return [swapped(piece, mask) for piece, mask in zip(pieces, masks)]

    other_weight = to_partner(out_weight)
    pairs = far_exchange(FAR, (0, 1))
    (near_stack,) = extract(
        place,
        sources,
        [(lambda p, i=i: p // NEAR * NEAR + i, (0, 1, 2)) for i in range(NEAR)],
        stacked=True,
    )
    near = exchanged(near_stack)
    held = attend(near, (NEAR, 0, NEAR, 0), finish=False, after=[other_weight], cost=COST[0])
    queries_far = []
    for mask in FAR:
        queries_far += far_exchange((mask,), (2,), [held[0], *pairs])
    (near_out,) = attend(near, (NEAR, 0, 0, NEAR), pairs=pairs, held=held, cost=COST[1])
    near_own = exchanged(near_out)
    own, last = [], near_out
    for i, mask in enumerate(FAR):
        (last,) = attend(
            near,
            (0, 1, NEAR, NEAR),
            queries=queries_far[i : i + 1],
            pairs=pairs,
            after=[last] + queries_far[i + 1 : i + 2],
            cost=COST[2 + i],
        )
        own.append(swapped(last, mask))
    near_other = to_partner(near_own)
    early_own = joined(own[:-1], [last])
    early_other = to_partner(early_own)
    weights = (out_weight, other_weight)
    before = gather_heads(
        place,
        core,
        [lambda p, i=i: p // NEAR * NEAR + i for i in range(NEAR)]
        + [lambda p, m=mask: p ^ m for mask in FAR[:-1]],
        [(near_own, i) for i in range(NEAR)] + [(early_own, i) for i in range(NEAR - 1)],
        [(near_other, i) for i in range(NEAR)] + [(early_other, i) for i in range(NEAR - 1)],
        *weights,
    )
    late_own = joined(own[-1:], [before])
    return finish(
        place, core, lambda p: p ^ FAR[-1], late_own, to_partner(late_own), *weights, before, residual, gate
    )


def absorb(state, block_pair, query_local):
    running, totals, accum = state
    rows_here = query_local.shape[0]
    heads_here = query_local.shape[1]
    key_block = block_pair[0].reshape(rows_here, heads_here, HEAD_DIM)
    value_block = block_pair[1].reshape(rows_here, heads_here, HEAD_DIM)
    scores = jnp.einsum(
        "qhd,khd->hqk", query_local, key_block, preferred_element_type=jnp.float32
    ) * (1.0 / HEAD_DIM**0.5)
    newmax = jnp.maximum(running, jnp.max(scores, axis=-1))
    correction = jnp.exp(running - newmax)
    weights = jnp.exp(scores - newmax[:, :, None])
    totals = totals * correction + jnp.sum(weights, axis=-1)
    update = jnp.einsum(
        "hqk,khd->qhd",
        weights.astype(jnp.bfloat16),
        value_block,
        preferred_element_type=jnp.float32,
    )
    accum = accum * correction.T[:, :, None] + update
    return (newmax, totals, accum)


def by_ring(queries, keys, values):
    rows_here = queries.shape[0]
    heads_here = queries.shape[1] // HEAD_DIM
    groups = lax.axis_size("ctx") // CYCLE
    query_local = queries.reshape(rows_here, heads_here, HEAD_DIM)
    own_pair = jnp.stack((keys, values))
    start_state = (
        jnp.full((heads_here, rows_here), -1e30, jnp.float32),
        jnp.zeros((heads_here, rows_here), jnp.float32),
        jnp.zeros((rows_here, heads_here, HEAD_DIM), jnp.float32),
    )
    state = absorb(start_state, own_pair, query_local)

    def both_step(counter, carry):
        inner, upward, downward = carry
        upward = passed_along(upward, "ctx", groups)
        downward = passed_along(downward, "ctx", -groups)
        inner = absorb(absorb(inner, upward, query_local), downward, query_local)
        return (inner, upward, downward)

    state, upward, _ = lax.fori_loop(0, CYCLE // 2 - 1, both_step, (state, own_pair, own_pair))
    opposite = passed_along(upward, "ctx", groups)
    state = absorb(state, opposite, query_local)
    running, totals, accum = state
    return (
        (accum / totals.T[:, :, None])
        .astype(jnp.bfloat16)
        .reshape(rows_here, heads_here * HEAD_DIM)
    )


def local(queries, keys, values, residual, gate, out_weight):
    if queries.shape[1] == CYCLE * HEAD_DIM and lax.axis_size("tp") == 2:
        return by_heads(queries, keys, values, residual, gate, out_weight)
    projected = lax.psum_scatter(
        lax.dot_general(
            out_weight,
            by_ring(queries, keys, values),
            (((0,), (1,)), ((), ())),
            preferred_element_type=jnp.float32,
        ).astype(jnp.bfloat16),
        "tp",
        scatter_dimension=0,
        tiled=True,
    ).astype(jnp.float32)
    return (residual.astype(jnp.float32) + gate[None, :] * projected.T).astype(jnp.bfloat16)


def solution(mesh):
    return jax.shard_map(
        local,
        mesh=mesh,
        in_specs=(
            P("ctx", "tp"),
            P("ctx", "tp"),
            P("ctx", "tp"),
            P("ctx", "tp"),
            P("tp"),
            P("tp", None),
        ),
        out_specs=P("ctx", "tp"),
        check_vma=False,
    )
```

```python
import functools
import math

import jax
import jax.numpy as jnp
from jax import lax
from jax.experimental import pallas as pl
from jax.experimental.pallas import tpu as pltpu
from jax.sharding import PartitionSpec as P

HEAD_DIM = 128
CYCLE = 8
NEAR = CYCLE // 2
FAR = (4, 5, 6, 7)
SCALE = math.log2(math.e) / math.sqrt(HEAD_DIM)
MIB = 2**20
LIMIT = (26, 26, 20)
COST = (2, 10, 10, 10)


def passed_along(array, axis, by):
    length = lax.axis_size(axis)
    return lax.ppermute(array, axis, [(i, (i + by) % length) for i in range(length)])


def swapped(array, mask):
    length = lax.axis_size("ctx")
    groups = length // CYCLE
    pairs = [(i, ((i // groups) ^ mask) * groups + i % groups) for i in range(length)]
    return lax.ppermute(array, "ctx", pairs)


def dot_nt(a, b):
    return lax.dot_general(a, b, (((1,), (1,)), ((), ())), preferred_element_type=jnp.float32)


def dot_nn(a, b):
    return lax.dot_general(a, b, (((1,), (0,)), ((), ())), preferred_element_type=jnp.float32)


def split_kernel(place_ref, queries, keys, values, near, *far):
    def columns(ref, head):
        return ref[:, pl.ds(pl.multiple_of(head * HEAD_DIM, HEAD_DIM), HEAD_DIM)]

    place = place_ref[0]
    for mask, out in zip(FAR, far):
        out[:, :HEAD_DIM] = columns(keys, place ^ mask)
        out[:, HEAD_DIM:] = columns(values, place ^ mask)
    for i in range(NEAR):
        for slot, ref in enumerate((keys, values, queries)):
            near[i, :, slot * HEAD_DIM : (slot + 1) * HEAD_DIM] = columns(ref, place // NEAR * NEAR + i)


def split_heads(place, queries, keys, values):
    rows, width = queries.shape
    tile = rows // 4
    return pl.pallas_call(
        split_kernel,
        name="split_heads",
        grid_spec=pltpu.PrefetchScalarGridSpec(
            num_scalar_prefetch=1,
            grid=(4,),
            in_specs=[pl.BlockSpec((tile, width), lambda i, place: (i, 0))] * 3,
            out_specs=[pl.BlockSpec((NEAR, tile, 3 * HEAD_DIM), lambda i, place: (0, i, 0))]
            + [pl.BlockSpec((tile, 2 * HEAD_DIM), lambda i, place: (i, 0))] * len(FAR),
        ),
        out_shape=[jax.ShapeDtypeStruct((NEAR, rows, 3 * HEAD_DIM), jnp.bfloat16)]
        + [jax.ShapeDtypeStruct((rows, 2 * HEAD_DIM), jnp.bfloat16)] * len(FAR),
        cost_estimate=pl.CostEstimate(flops=0, bytes_accessed=0, transcendentals=0),
        compiler_params=pltpu.CompilerParams(vmem_limit_bytes=56 * MIB),
    )(place, queries, keys, values)


def heads_kernel(place_ref, *refs):
    for i in range(len(FAR)):
        refs[i - len(FAR)][...] = refs[i][...]


def far_heads(place, queries, after):
    rows = queries.shape[0]
    return pl.pallas_call(
        heads_kernel,
        name="far_heads",
        grid_spec=pltpu.PrefetchScalarGridSpec(
            num_scalar_prefetch=1,
            grid=(1,),
            in_specs=[
                pl.BlockSpec((rows, HEAD_DIM), lambda i, place, m=mask: (0, place[0] ^ m)) for mask in FAR
            ]
            + [pl.BlockSpec(memory_space=pl.ANY)] * len(after),
            out_specs=[pl.BlockSpec((rows, HEAD_DIM), lambda i, place: (0, 0))] * len(FAR),
        ),
        out_shape=[jax.ShapeDtypeStruct((rows, HEAD_DIM), jnp.bfloat16)] * len(FAR),
        cost_estimate=pl.CostEstimate(flops=0, bytes_accessed=0, transcendentals=0),
        compiler_params=pltpu.CompilerParams(vmem_limit_bytes=16 * MIB),
    )(place, *[queries] * len(FAR), *after)


def fill(kd, vx, i, pair):
    rows = pair.shape[0]
    span = pl.ds(i * rows, rows)
    kd[span, :HEAD_DIM] = pair[:, :HEAD_DIM]
    kd[span, HEAD_DIM:] = pair[:, :HEAD_DIM]
    vx[span, :HEAD_DIM] = pair[:, HEAD_DIM : 2 * HEAD_DIM]
    vx[span, HEAD_DIM:] = jnp.ones((rows, HEAD_DIM), jnp.bfloat16)


def halves_of(query):
    scaled = query.astype(jnp.float32) * SCALE
    high = scaled.astype(jnp.bfloat16)
    return jnp.concatenate([high, (scaled - high.astype(jnp.float32)).astype(jnp.bfloat16)], axis=1)


def run_blocks(query, blocks, rows, top=None, total=None):
    upcoming = dot_nt(query, blocks[0][0][pl.ds(blocks[0][2], rows), :])
    for i, (_, vx, start) in enumerate(blocks):
        scores = upcoming
        if i + 1 < len(blocks):
            upcoming = dot_nt(query, blocks[i + 1][0][pl.ds(blocks[i + 1][2], rows), :])
        largest = jnp.max(scores, axis=1, keepdims=True)
        newtop = largest if top is None else jnp.maximum(top, largest)
        weights = jnp.exp2(scores - newtop).astype(jnp.bfloat16)
        update = dot_nn(weights, vx[pl.ds(start, rows), :])
        total = update if top is None else total * jnp.exp2(top - newtop) + update
        top = newtop
    return top, total


def blocks_of(rows, *pairs):
    return [(kd, vx, i * rows) for kd, vx in pairs for i in range(NEAR)]


def divided(total):
    return (total[:, :HEAD_DIM] / total[:, HEAD_DIM:]).astype(jnp.bfloat16)


def near_kernel(near, weight, tops, totals, split, near_pair, kd, vx):
    rows = near.shape[1]
    for i in range(NEAR):
        split[i] = halves_of(near[i, :, 2 * HEAD_DIM :])
        near_pair[i] = near[i, :, : 2 * HEAD_DIM]
        fill(kd, vx, i, near.at[i])

    def one_query(j, carry):
        top, totals[j] = run_blocks(split[j], blocks_of(rows, (kd, vx)), rows)
        tops[j] = jnp.broadcast_to(top, (rows, HEAD_DIM))
        return carry

    lax.fori_loop(0, NEAR, one_query, 0)


def rest_kernel(tops, totals, split, *refs):
    pairs, (out, kd, vx) = refs[:NEAR], refs[NEAR:]
    rows = split.shape[1]
    for i, pair in enumerate(pairs):
        fill(kd, vx, i, pair)

    def one_query(j, carry):
        top = jnp.max(tops[j], axis=1, keepdims=True)
        out[j] = divided(run_blocks(split[j], blocks_of(rows, (kd, vx)), rows, top, totals[j])[1])
        return carry

    lax.fori_loop(0, NEAR, one_query, 0)


def whole_kernel(query, near_pair, *refs):
    pairs, (out, kd, vx) = refs[:NEAR], refs[-3:]
    rows = query.shape[0]
    for i in range(NEAR):
        fill(kd, vx, i, near_pair.at[i])
        fill(kd, vx, NEAR + i, pairs[i])
    blocks = [(kd, vx, i * rows) for i in range(CYCLE)]
    out[0] = divided(run_blocks(halves_of(query[...]), blocks, rows)[1])


def vmem_call(kernel, name, shapes, count, limit, operands, after=(), cost=0):
    return pl.pallas_call(
        kernel,
        name=name,
        out_shape=[jax.ShapeDtypeStruct(shape, dtype) for shape, dtype in shapes],
        in_specs=[pl.BlockSpec(memory_space=pltpu.VMEM)] * len(operands)
        + [pl.BlockSpec(memory_space=pl.ANY)] * len(after),
        scratch_shapes=[pltpu.VMEM((count * operands[-1].shape[-2], 2 * HEAD_DIM), jnp.bfloat16)] * 2,
        compiler_params=pltpu.CompilerParams(vmem_limit_bytes=limit * MIB),
        cost_estimate=pl.CostEstimate(flops=cost * 10**9, bytes_accessed=0, transcendentals=0),
    )(*operands, *after)


def attend_near(near, after):
    rows = near.shape[1]
    shape = (NEAR, rows, 2 * HEAD_DIM)
    shapes = [((NEAR, rows, HEAD_DIM), jnp.float32), (shape, jnp.float32)] + [(shape, jnp.bfloat16)] * 2
    return vmem_call(near_kernel, "attend_near", shapes, NEAR, LIMIT[0], [near], after)


def attend_rest(tops, totals, split, pairs):
    shapes = [((NEAR, split.shape[1], HEAD_DIM), jnp.bfloat16)]
    return vmem_call(rest_kernel, "attend_rest", shapes, NEAR, LIMIT[1], [tops, totals, split, *pairs])[0]


def attend_whole(query, near_pair, pairs, after, cost):
    shapes = [((1, *query.shape), jnp.bfloat16)]
    operands = [query, near_pair, *pairs]
    return vmem_call(whole_kernel, "attend_whole", shapes, CYCLE, LIMIT[2], operands, after, cost)[0]


def gather_kernel(heads, place_ref, core_ref, *refs):
    count = len(heads)
    own, other, (own_weight, other_weight, out, token) = refs[:count], refs[count : 2 * count], refs[2 * count :]
    left = jnp.concatenate([piece[...] for piece in own + other], axis=1)
    starts = [pl.multiple_of(head(place_ref[0]) * HEAD_DIM, HEAD_DIM) for head in heads]
    right = jnp.concatenate(
        [weight[pl.ds(start, HEAD_DIM), :] for weight in (own_weight, other_weight) for start in starts],
        axis=0,
    )
    out[...] = dot_nn(left, right).astype(out.dtype)
    token[...] = jnp.zeros_like(token)


def gather_heads(place, core, heads, own, other, out_weight, other_weight):
    rows, width = own[0][0].shape[1], out_weight.shape[1] // 2
    tile = width // 3
    pieces = [*own, *other]
    weight_spec = pl.BlockSpec(
        (out_weight.shape[0], tile), lambda c, place, core: (0, core[0] * 3 + c)
    )
    return pl.pallas_call(
        functools.partial(gather_kernel, heads),
        name="gather_heads",
        grid_spec=pltpu.PrefetchScalarGridSpec(
            num_scalar_prefetch=2,
            grid=(3,),
            in_specs=[
                pl.BlockSpec((None, rows, HEAD_DIM), lambda c, place, core, n=index: (n, 0, 0))
                for _, index in pieces
            ]
            + [weight_spec] * 2,
            out_specs=[
                pl.BlockSpec((rows, tile), lambda c, place, core: (0, c)),
                pl.BlockSpec((8, HEAD_DIM), lambda c, place, core: (0, 0)),
            ],
        ),
        out_shape=[
            jax.ShapeDtypeStruct((rows, width), jnp.bfloat16),
            jax.ShapeDtypeStruct((8, HEAD_DIM), jnp.float32),
        ],
        compiler_params=pltpu.CompilerParams(vmem_limit_bytes=32 * MIB),
        cost_estimate=pl.CostEstimate(flops=0, bytes_accessed=0, transcendentals=0),
    )(place, core, *[array for array, _ in pieces], out_weight, other_weight)


def finish_kernel(place_ref, core_ref, own, other, own_rows, other_rows, before, residual, gate, out):
    left = jnp.concatenate([own[...], other[...]], axis=1)
    right = jnp.concatenate([own_rows[...], other_rows[...]], axis=0)
    total = before[...].astype(jnp.float32) + dot_nn(left, right)
    out[...] = (residual[...].astype(jnp.float32) + gate[...] * total).astype(out.dtype)


def finish(place, core, head, own, other, out_weight, other_weight, before, residual, gate):
    rows, width = residual.shape
    tile = rows // 4
    piece = pl.BlockSpec((None, tile, HEAD_DIM), lambda i, place, core: (0, i, 0))
    weight_rows = pl.BlockSpec((HEAD_DIM, width), lambda i, place, core: (head(place[0]), core[0]))
    tiled = pl.BlockSpec((tile, width), lambda i, place, core: (i, 0))
    return pl.pallas_call(
        finish_kernel,
        name="finish",
        grid_spec=pltpu.PrefetchScalarGridSpec(
            num_scalar_prefetch=2,
            grid=(4,),
            in_specs=[piece] * 2
            + [weight_rows] * 2
            + [tiled] * 2
            + [pl.BlockSpec((1, width), lambda i, place, core: (0, 0))],
            out_specs=tiled,
        ),
        out_shape=jax.ShapeDtypeStruct((rows, width), jnp.bfloat16),
        compiler_params=pltpu.CompilerParams(vmem_limit_bytes=16 * MIB),
        cost_estimate=pl.CostEstimate(flops=0, bytes_accessed=0, transcendentals=0),
    )(place, core, own, other, out_weight, other_weight, before, residual, gate.reshape(1, -1))


def joined_kernel(count, *refs):
    for i in range(count):
        refs[-1][i] = refs[i][0]


def joined(pieces, after):
    shape = (len(pieces), *pieces[0].shape[1:])
    return pl.pallas_call(
        functools.partial(joined_kernel, len(pieces)),
        name="joined",
        in_specs=[pl.BlockSpec(memory_space=pltpu.VMEM)] * len(pieces)
        + [pl.BlockSpec(memory_space=pl.ANY)] * len(after),
        out_shape=jax.ShapeDtypeStruct(shape, pieces[0].dtype),
        compiler_params=pltpu.CompilerParams(vmem_limit_bytes=16 * MIB),
        cost_estimate=pl.CostEstimate(flops=0, bytes_accessed=0, transcendentals=0),
    )(*pieces, *after)


def to_partner(array):
    return lax.ppermute(array, "tp", [(0, 1), (1, 0)])


def by_heads(queries, keys, values, residual, gate, out_weight):
    length = lax.axis_size("ctx")
    groups = length // CYCLE
    place = (lax.axis_index("ctx") // groups).reshape(1).astype(jnp.int32)
    core = lax.axis_index("tp").reshape(1).astype(jnp.int32)
    near_groups = [
        [(half * NEAR + i) * groups + g for i in range(NEAR)] for half in (0, 1) for g in range(groups)
    ]

    def exchanged(array):
        return lax.all_to_all(array, "ctx", 0, 0, axis_index_groups=near_groups, tiled=True)

    other_weight = to_partner(out_weight)
    near_stack, *far_pairs = split_heads(place, queries, keys, values)
    pairs = [swapped(pair, mask) for pair, mask in zip(far_pairs, FAR)]
    near = exchanged(near_stack)
    tops, totals, split, near_pair = attend_near(near, [other_weight])
    far_queries = far_heads(place, queries, [tops, *pairs])
    far_queries = [swapped(query, mask) for query, mask in zip(far_queries, FAR)]
    near_out = attend_rest(tops, totals, split, pairs)
    near_own = exchanged(near_out)
    own, last = [], near_out
    for i, mask in enumerate(FAR):
        last = attend_whole(
            far_queries[i], near_pair, pairs, [last] + far_queries[i + 1 : i + 2], COST[i]
        )
        own.append(swapped(last, mask))
    near_other = to_partner(near_own)
    early_own = joined(own[:-1], [last])
    early_other = to_partner(early_own)
    weights = (out_weight, other_weight)
    before, token = gather_heads(
        place,
        core,
        [lambda p, i=i: p // NEAR * NEAR + i for i in range(NEAR)]
        + [lambda p, m=mask: p ^ m for mask in FAR[:-1]],
        [(near_own, i) for i in range(NEAR)] + [(early_own, i) for i in range(NEAR - 1)],
        [(near_other, i) for i in range(NEAR)] + [(early_other, i) for i in range(NEAR - 1)],
        *weights,
    )
    late_own = joined(own[-1:], [token])
    return finish(
        place, core, lambda p: p ^ FAR[-1], late_own, to_partner(late_own), *weights, before, residual, gate
    )


def absorb(state, block_pair, query_local):
    running, totals, accum = state
    rows_here = query_local.shape[0]
    heads_here = query_local.shape[1]
    key_block = block_pair[0].reshape(rows_here, heads_here, HEAD_DIM)
    value_block = block_pair[1].reshape(rows_here, heads_here, HEAD_DIM)
    scores = jnp.einsum(
        "qhd,khd->hqk", query_local, key_block, preferred_element_type=jnp.float32
    ) * (1.0 / HEAD_DIM**0.5)
    newmax = jnp.maximum(running, jnp.max(scores, axis=-1))
    correction = jnp.exp(running - newmax)
    weights = jnp.exp(scores - newmax[:, :, None])
    totals = totals * correction + jnp.sum(weights, axis=-1)
    update = jnp.einsum(
        "hqk,khd->qhd",
        weights.astype(jnp.bfloat16),
        value_block,
        preferred_element_type=jnp.float32,
    )
    accum = accum * correction.T[:, :, None] + update
    return (newmax, totals, accum)


def by_ring(queries, keys, values):
    rows_here = queries.shape[0]
    heads_here = queries.shape[1] // HEAD_DIM
    groups = lax.axis_size("ctx") // CYCLE
    query_local = queries.reshape(rows_here, heads_here, HEAD_DIM)
    own_pair = jnp.stack((keys, values))
    start_state = (
        jnp.full((heads_here, rows_here), -1e30, jnp.float32),
        jnp.zeros((heads_here, rows_here), jnp.float32),
        jnp.zeros((rows_here, heads_here, HEAD_DIM), jnp.float32),
    )
    state = absorb(start_state, own_pair, query_local)

    def both_step(counter, carry):
        inner, upward, downward = carry
        upward = passed_along(upward, "ctx", groups)
        downward = passed_along(downward, "ctx", -groups)
        inner = absorb(absorb(inner, upward, query_local), downward, query_local)
        return (inner, upward, downward)

    state, upward, _ = lax.fori_loop(0, CYCLE // 2 - 1, both_step, (state, own_pair, own_pair))
    opposite = passed_along(upward, "ctx", groups)
    state = absorb(state, opposite, query_local)
    running, totals, accum = state
    return (
        (accum / totals.T[:, :, None])
        .astype(jnp.bfloat16)
        .reshape(rows_here, heads_here * HEAD_DIM)
    )


def local(queries, keys, values, residual, gate, out_weight):
    if queries.shape[1] == CYCLE * HEAD_DIM and lax.axis_size("tp") == 2:
        return by_heads(queries, keys, values, residual, gate, out_weight)
    projected = lax.psum_scatter(
        lax.dot_general(
            out_weight,
            by_ring(queries, keys, values),
            (((0,), (1,)), ((), ())),
            preferred_element_type=jnp.float32,
        ).astype(jnp.bfloat16),
        "tp",
        scatter_dimension=0,
        tiled=True,
    ).astype(jnp.float32)
    return (residual.astype(jnp.float32) + gate[None, :] * projected.T).astype(jnp.bfloat16)


def solution(mesh):
    return jax.shard_map(
        local,
        mesh=mesh,
        in_specs=(
            P("ctx", "tp"),
            P("ctx", "tp"),
            P("ctx", "tp"),
            P("ctx", "tp"),
            P("tp"),
            P("tp", None),
        ),
        out_specs=P("ctx", "tp"),
        check_vma=False,
    )
```

```python
import functools
import math

import jax
import jax.numpy as jnp
from jax import lax
from jax.experimental import pallas as pl
from jax.experimental.pallas import tpu as pltpu
from jax.sharding import PartitionSpec as P

HEAD_DIM = 128
CYCLE = 8
NEAR = CYCLE // 2
FAR = (7, 6, 5, 4)
SCALE = math.log2(math.e) / math.sqrt(HEAD_DIM)
MIB = 2**20
LIMIT = (20, 20, 18)
COST = (2, 10, 10, 10)


def passed_along(array, axis, by):
    length = lax.axis_size(axis)
    return lax.ppermute(array, axis, [(i, (i + by) % length) for i in range(length)])


def swapped(array, mask):
    length = lax.axis_size("ctx")
    groups = length // CYCLE
    pairs = [(i, ((i // groups) ^ mask) * groups + i % groups) for i in range(length)]
    return lax.ppermute(array, "ctx", pairs)


def dot_nt(a, b):
    return lax.dot_general(a, b, (((1,), (1,)), ((), ())), preferred_element_type=jnp.float32)


def dot_nn(a, b):
    return lax.dot_general(a, b, (((1,), (0,)), ((), ())), preferred_element_type=jnp.float32)


def split_kernel(place_ref, queries, keys, values, near, *far):
    def columns(ref, head):
        return ref[:, pl.ds(pl.multiple_of(head * HEAD_DIM, HEAD_DIM), HEAD_DIM)]

    place = place_ref[0]
    for mask, out in zip(FAR, far):
        out[:, :HEAD_DIM] = columns(keys, place ^ mask)
        out[:, HEAD_DIM:] = columns(values, place ^ mask)
    for i in range(NEAR):
        for slot, ref in enumerate((keys, values, queries)):
            near[i, :, slot * HEAD_DIM : (slot + 1) * HEAD_DIM] = columns(ref, place // NEAR * NEAR + i)


def split_heads(place, queries, keys, values):
    rows, width = queries.shape
    tile = rows // 4
    return pl.pallas_call(
        split_kernel,
        name="split_heads",
        grid_spec=pltpu.PrefetchScalarGridSpec(
            num_scalar_prefetch=1,
            grid=(4,),
            in_specs=[pl.BlockSpec((tile, width), lambda i, place: (i, 0))] * 3,
            out_specs=[pl.BlockSpec((NEAR, tile, 3 * HEAD_DIM), lambda i, place: (0, i, 0))]
            + [pl.BlockSpec((tile, 2 * HEAD_DIM), lambda i, place: (i, 0))] * len(FAR),
        ),
        out_shape=[jax.ShapeDtypeStruct((NEAR, rows, 3 * HEAD_DIM), jnp.bfloat16)]
        + [jax.ShapeDtypeStruct((rows, 2 * HEAD_DIM), jnp.bfloat16)] * len(FAR),
        cost_estimate=pl.CostEstimate(flops=0, bytes_accessed=0, transcendentals=0),
        compiler_params=pltpu.CompilerParams(vmem_limit_bytes=56 * MIB),
    )(place, queries, keys, values)


def heads_kernel(place_ref, *refs):
    for i in range(len(FAR)):
        refs[i - len(FAR)][...] = refs[i][...]


def far_heads(place, queries, after):
    rows = queries.shape[0]
    return pl.pallas_call(
        heads_kernel,
        name="far_heads",
        grid_spec=pltpu.PrefetchScalarGridSpec(
            num_scalar_prefetch=1,
            grid=(1,),
            in_specs=[
                pl.BlockSpec((rows, HEAD_DIM), lambda i, place, m=mask: (0, place[0] ^ m)) for mask in FAR
            ]
            + [pl.BlockSpec(memory_space=pl.ANY)] * len(after),
            out_specs=[pl.BlockSpec((rows, HEAD_DIM), lambda i, place: (0, 0))] * len(FAR),
        ),
        out_shape=[jax.ShapeDtypeStruct((rows, HEAD_DIM), jnp.bfloat16)] * len(FAR),
        cost_estimate=pl.CostEstimate(flops=0, bytes_accessed=0, transcendentals=0),
        compiler_params=pltpu.CompilerParams(vmem_limit_bytes=16 * MIB),
    )(place, *[queries] * len(FAR), *after)


def fill(kd, vx, i, pair):
    rows = pair.shape[0]
    span = pl.ds(i * rows, rows)
    kd[span, :HEAD_DIM] = pair[:, :HEAD_DIM]
    kd[span, HEAD_DIM:] = pair[:, :HEAD_DIM]
    vx[span, :HEAD_DIM] = pair[:, HEAD_DIM : 2 * HEAD_DIM]
    vx[span, HEAD_DIM:] = jnp.ones((rows, HEAD_DIM), jnp.bfloat16)


def halves_of(query):
    scaled = query.astype(jnp.float32) * SCALE
    high = scaled.astype(jnp.bfloat16)
    return jnp.concatenate([high, (scaled - high.astype(jnp.float32)).astype(jnp.bfloat16)], axis=1)


def run_blocks(query, blocks, rows, top=None, total=None):
    upcoming = dot_nt(query, blocks[0][0][pl.ds(blocks[0][2], rows), :])
    for i, (_, vx, start) in enumerate(blocks):
        scores = upcoming
        if i + 1 < len(blocks):
            upcoming = dot_nt(query, blocks[i + 1][0][pl.ds(blocks[i + 1][2], rows), :])
        largest = jnp.max(scores, axis=1, keepdims=True)
        newtop = largest if top is None else jnp.maximum(top, largest)
        weights = jnp.exp2(scores - newtop).astype(jnp.bfloat16)
        update = dot_nn(weights, vx[pl.ds(start, rows), :])
        total = update if top is None else total * jnp.exp2(top - newtop) + update
        top = newtop
    return top, total


def blocks_of(rows, *pairs):
    return [(kd, vx, i * rows) for kd, vx in pairs for i in range(NEAR)]


def divided(total):
    return (total[:, :HEAD_DIM] / total[:, HEAD_DIM:]).astype(jnp.bfloat16)


def near_kernel(near, weight, tops, totals, split, near_pair, kd, vx):
    rows = near.shape[1]
    for i in range(NEAR):
        split[i] = halves_of(near[i, :, 2 * HEAD_DIM :])
        near_pair[i] = near[i, :, : 2 * HEAD_DIM]
        fill(kd, vx, i, near.at[i])

    def one_query(j, carry):
        top, totals[j] = run_blocks(split[j], blocks_of(rows, (kd, vx)), rows)
        tops[j] = jnp.broadcast_to(top, (rows, HEAD_DIM))
        return carry

    lax.fori_loop(0, NEAR, one_query, 0)


def rest_kernel(tops, totals, split, *refs):
    pairs, (out, kd, vx) = refs[:NEAR], refs[NEAR:]
    rows = split.shape[1]
    for i, pair in enumerate(pairs):
        fill(kd, vx, i, pair)

    def one_query(j, carry):
        top = jnp.max(tops[j], axis=1, keepdims=True)
        out[j] = divided(run_blocks(split[j], blocks_of(rows, (kd, vx)), rows, top, totals[j])[1])
        return carry

    lax.fori_loop(0, NEAR, one_query, 0)


def whole_kernel(query, near_pair, *refs):
    pairs, (out, kd, vx) = refs[:NEAR], refs[-3:]
    rows = query.shape[0]
    for i in range(NEAR):
        fill(kd, vx, i, near_pair.at[i])
        fill(kd, vx, NEAR + i, pairs[i])
    blocks = [(kd, vx, i * rows) for i in range(CYCLE)]
    out[0] = divided(run_blocks(halves_of(query[...]), blocks, rows)[1])


def vmem_call(kernel, name, shapes, count, limit, operands, after=(), cost=0):
    return pl.pallas_call(
        kernel,
        name=name,
        out_shape=[jax.ShapeDtypeStruct(shape, dtype) for shape, dtype in shapes],
        in_specs=[pl.BlockSpec(memory_space=pltpu.VMEM)] * len(operands)
        + [pl.BlockSpec(memory_space=pl.ANY)] * len(after),
        scratch_shapes=[pltpu.VMEM((count * operands[-1].shape[-2], 2 * HEAD_DIM), jnp.bfloat16)] * 2,
        compiler_params=pltpu.CompilerParams(vmem_limit_bytes=limit * MIB),
        cost_estimate=pl.CostEstimate(flops=cost * 10**9, bytes_accessed=0, transcendentals=0),
    )(*operands, *after)


def attend_near(near, after):
    rows = near.shape[1]
    shape = (NEAR, rows, 2 * HEAD_DIM)
    shapes = [((NEAR, rows, HEAD_DIM), jnp.float32), (shape, jnp.float32)] + [(shape, jnp.bfloat16)] * 2
    return vmem_call(near_kernel, "attend_near", shapes, NEAR, LIMIT[0], [near], after)


def attend_rest(tops, totals, split, pairs):
    shapes = [((NEAR, split.shape[1], HEAD_DIM), jnp.bfloat16)]
    return vmem_call(rest_kernel, "attend_rest", shapes, NEAR, LIMIT[1], [tops, totals, split, *pairs])[0]


def attend_whole(query, near_pair, pairs, after, cost):
    shapes = [((1, *query.shape), jnp.bfloat16)]
    operands = [query, near_pair, *pairs]
    return vmem_call(whole_kernel, "attend_whole", shapes, CYCLE, LIMIT[2], operands, after, cost)[0]


def gather_kernel(heads, place_ref, core_ref, *refs):
    count = len(heads)
    own, other, (own_weight, other_weight, out, token) = refs[:count], refs[count : 2 * count], refs[2 * count :]
    left = jnp.concatenate([piece[...] for piece in own + other], axis=1)
    starts = [pl.multiple_of(head(place_ref[0]) * HEAD_DIM, HEAD_DIM) for head in heads]
    right = jnp.concatenate(
        [weight[pl.ds(start, HEAD_DIM), :] for weight in (own_weight, other_weight) for start in starts],
        axis=0,
    )
    out[...] = dot_nn(left, right).astype(out.dtype)
    token[...] = jnp.zeros_like(token)


def gather_heads(place, core, heads, own, other, out_weight, other_weight):
    rows, width = own[0][0].shape[1], out_weight.shape[1] // 2
    tile = width // 3
    pieces = [*own, *other]
    weight_spec = pl.BlockSpec(
        (out_weight.shape[0], tile), lambda c, place, core: (0, core[0] * 3 + c)
    )
    return pl.pallas_call(
        functools.partial(gather_kernel, heads),
        name="gather_heads",
        grid_spec=pltpu.PrefetchScalarGridSpec(
            num_scalar_prefetch=2,
            grid=(3,),
            in_specs=[
                pl.BlockSpec((None, rows, HEAD_DIM), lambda c, place, core, n=index: (n, 0, 0))
                for _, index in pieces
            ]
            + [weight_spec] * 2,
            out_specs=[
                pl.BlockSpec((rows, tile), lambda c, place, core: (0, c)),
                pl.BlockSpec((8, HEAD_DIM), lambda c, place, core: (0, 0)),
            ],
        ),
        out_shape=[
            jax.ShapeDtypeStruct((rows, width), jnp.bfloat16),
            jax.ShapeDtypeStruct((8, HEAD_DIM), jnp.float32),
        ],
        compiler_params=pltpu.CompilerParams(vmem_limit_bytes=32 * MIB),
        cost_estimate=pl.CostEstimate(flops=0, bytes_accessed=0, transcendentals=0),
    )(place, core, *[array for array, _ in pieces], out_weight, other_weight)


def finish_kernel(place_ref, core_ref, own, other, own_rows, other_rows, before, residual, gate, out):
    left = jnp.concatenate([own[...], other[...]], axis=1)
    right = jnp.concatenate([own_rows[...], other_rows[...]], axis=0)
    total = before[...].astype(jnp.float32) + dot_nn(left, right)
    out[...] = (residual[...].astype(jnp.float32) + gate[...] * total).astype(out.dtype)


def finish(place, core, head, own, other, out_weight, other_weight, before, residual, gate):
    rows, width = residual.shape
    tile = rows // 4
    piece = pl.BlockSpec((None, tile, HEAD_DIM), lambda i, place, core: (0, i, 0))
    weight_rows = pl.BlockSpec((HEAD_DIM, width), lambda i, place, core: (head(place[0]), core[0]))
    tiled = pl.BlockSpec((tile, width), lambda i, place, core: (i, 0))
    return pl.pallas_call(
        finish_kernel,
        name="finish",
        grid_spec=pltpu.PrefetchScalarGridSpec(
            num_scalar_prefetch=2,
            grid=(4,),
            in_specs=[piece] * 2
            + [weight_rows] * 2
            + [tiled] * 2
            + [pl.BlockSpec((1, width), lambda i, place, core: (0, 0))],
            out_specs=tiled,
        ),
        out_shape=jax.ShapeDtypeStruct((rows, width), jnp.bfloat16),
        compiler_params=pltpu.CompilerParams(vmem_limit_bytes=16 * MIB),
        cost_estimate=pl.CostEstimate(flops=0, bytes_accessed=0, transcendentals=0),
    )(place, core, own, other, out_weight, other_weight, before, residual, gate.reshape(1, -1))


def joined_kernel(count, *refs):
    for i in range(count):
        refs[-1][i] = refs[i][0]


def joined(pieces, after):
    shape = (len(pieces), *pieces[0].shape[1:])
    return pl.pallas_call(
        functools.partial(joined_kernel, len(pieces)),
        name="joined",
        in_specs=[pl.BlockSpec(memory_space=pltpu.VMEM)] * len(pieces)
        + [pl.BlockSpec(memory_space=pl.ANY)] * len(after),
        out_shape=jax.ShapeDtypeStruct(shape, pieces[0].dtype),
        compiler_params=pltpu.CompilerParams(vmem_limit_bytes=16 * MIB),
        cost_estimate=pl.CostEstimate(flops=0, bytes_accessed=0, transcendentals=0),
    )(*pieces, *after)


def to_partner(array):
    return lax.ppermute(array, "tp", [(0, 1), (1, 0)])


def by_heads(queries, keys, values, residual, gate, out_weight):
    length = lax.axis_size("ctx")
    groups = length // CYCLE
    place = (lax.axis_index("ctx") // groups).reshape(1).astype(jnp.int32)
    core = lax.axis_index("tp").reshape(1).astype(jnp.int32)
    near_groups = [
        [(half * NEAR + i) * groups + g for i in range(NEAR)] for half in (0, 1) for g in range(groups)
    ]

    def exchanged(array):
        return lax.all_to_all(array, "ctx", 0, 0, axis_index_groups=near_groups, tiled=True)

    other_weight = to_partner(out_weight)
    near_stack, *far_pairs = split_heads(place, queries, keys, values)
    pairs = [swapped(pair, mask) for pair, mask in zip(far_pairs, FAR)]
    near = exchanged(near_stack)
    tops, totals, split, near_pair = attend_near(near, [other_weight])
    far_queries = far_heads(place, queries, [tops])
    far_queries = [swapped(query, mask) for query, mask in zip(far_queries, FAR)]
    near_out = attend_rest(tops, totals, split, pairs)
    near_own = exchanged(near_out)
    own, last = [], near_out
    for i, mask in enumerate(FAR):
        last = attend_whole(
            far_queries[i], near_pair, pairs, [last] + far_queries[i + 1 : i + 2], COST[i]
        )
        own.append(swapped(last, mask))
    near_other = to_partner(near_own)
    early_own = joined(own[:-1], [last])
    early_other = to_partner(early_own)
    weights = (out_weight, other_weight)
    before, token = gather_heads(
        place,
        core,
        [lambda p, i=i: p // NEAR * NEAR + i for i in range(NEAR)]
        + [lambda p, m=mask: p ^ m for mask in FAR[:-1]],
        [(near_own, i) for i in range(NEAR)] + [(early_own, i) for i in range(NEAR - 1)],
        [(near_other, i) for i in range(NEAR)] + [(early_other, i) for i in range(NEAR - 1)],
        *weights,
    )
    late_own = joined(own[-1:], [token])
    return finish(
        place, core, lambda p: p ^ FAR[-1], late_own, to_partner(late_own), *weights, before, residual, gate
    )


def absorb(state, block_pair, query_local):
    running, totals, accum = state
    rows_here = query_local.shape[0]
    heads_here = query_local.shape[1]
    key_block = block_pair[0].reshape(rows_here, heads_here, HEAD_DIM)
    value_block = block_pair[1].reshape(rows_here, heads_here, HEAD_DIM)
    scores = jnp.einsum(
        "qhd,khd->hqk", query_local, key_block, preferred_element_type=jnp.float32
    ) * (1.0 / HEAD_DIM**0.5)
    newmax = jnp.maximum(running, jnp.max(scores, axis=-1))
    correction = jnp.exp(running - newmax)
    weights = jnp.exp(scores - newmax[:, :, None])
    totals = totals * correction + jnp.sum(weights, axis=-1)
    update = jnp.einsum(
        "hqk,khd->qhd",
        weights.astype(jnp.bfloat16),
        value_block,
        preferred_element_type=jnp.float32,
    )
    accum = accum * correction.T[:, :, None] + update
    return (newmax, totals, accum)


def by_ring(queries, keys, values):
    rows_here = queries.shape[0]
    heads_here = queries.shape[1] // HEAD_DIM
    groups = lax.axis_size("ctx") // CYCLE
    query_local = queries.reshape(rows_here, heads_here, HEAD_DIM)
    own_pair = jnp.stack((keys, values))
    start_state = (
        jnp.full((heads_here, rows_here), -1e30, jnp.float32),
        jnp.zeros((heads_here, rows_here), jnp.float32),
        jnp.zeros((rows_here, heads_here, HEAD_DIM), jnp.float32),
    )
    state = absorb(start_state, own_pair, query_local)

    def both_step(counter, carry):
        inner, upward, downward = carry
        upward = passed_along(upward, "ctx", groups)
        downward = passed_along(downward, "ctx", -groups)
        inner = absorb(absorb(inner, upward, query_local), downward, query_local)
        return (inner, upward, downward)

    state, upward, _ = lax.fori_loop(0, CYCLE // 2 - 1, both_step, (state, own_pair, own_pair))
    opposite = passed_along(upward, "ctx", groups)
    state = absorb(state, opposite, query_local)
    running, totals, accum = state
    return (
        (accum / totals.T[:, :, None])
        .astype(jnp.bfloat16)
        .reshape(rows_here, heads_here * HEAD_DIM)
    )


def local(queries, keys, values, residual, gate, out_weight):
    if queries.shape[1] == CYCLE * HEAD_DIM and lax.axis_size("tp") == 2:
        return by_heads(queries, keys, values, residual, gate, out_weight)
    projected = lax.psum_scatter(
        lax.dot_general(
            out_weight,
            by_ring(queries, keys, values),
            (((0,), (1,)), ((), ())),
            preferred_element_type=jnp.float32,
        ).astype(jnp.bfloat16),
        "tp",
        scatter_dimension=0,
        tiled=True,
    ).astype(jnp.float32)
    return (residual.astype(jnp.float32) + gate[None, :] * projected.T).astype(jnp.bfloat16)


def solution(mesh):
    return jax.shard_map(
        local,
        mesh=mesh,
        in_specs=(
            P("ctx", "tp"),
            P("ctx", "tp"),
            P("ctx", "tp"),
            P("ctx", "tp"),
            P("tp"),
            P("tp", None),
        ),
        out_specs=P("ctx", "tp"),
        check_vma=False,
    )
```
